128 devices in a mesh: grp: 4 (over y_lo, core), mem: 32 (over x, z, y_hi).
Axes of the slice: x: 4, y: 4 (y_hi: 2, y_lo: 2; y = y_hi * 2 + y_lo), z: 4, core: 2. Of those that a mesh axis runs over, the one named last changes fastest.
Arguments:
- video: bfloat16 [128, 32, 32, 1024], P('mem', 'grp'), may hold values from -6 to 6
- w_triple: bfloat16 [2, 1024, 3072], replicated, may hold values from -0.75 to 0.75, as said below
- w_out: bfloat16 [2, 1024, 1024], replicated, may hold values from -0.1875 to 0.1875
Outputs:
- result: bfloat16 [128, 32, 32, 1024], P('mem', 'grp')
The draws below stay inside these ranges and needn't reach their ends.
Inputs may be any that keep to these rules, and one draw needn't show every extreme that they name: `w_triple`: entries of order 1024 ** -0.5, independent between columns of values.
All inputs are finite; a program needn't handle non-finite values.
Results may differ from the reference program's by a relative error of at most 0.008.
Values may be sent and summed in bfloat16 or wider, within the bound.
No kernel may reach another device: no remote copies, remote signals or barrier semaphores. Data moves between devices by JAX's collectives and lax.ppermute only.
A program may use at most 128 MiB of HBM per device.

```python
import jax
import jax.numpy as jnp
from jax import lax

D = 1024
HEADS = 16
HEAD = 64
COLS = 32
BLOCKS = 2
FRAMES = 128
ROWS = 32


def draw_video(key, part):
    base = jax.random.normal(key, (FRAMES, ROWS, COLS, D), jnp.float32)
    return jnp.clip(base, -6.0, 6.0).astype(jnp.bfloat16)


def draw_w_triple(key, part):
    weights = jax.random.truncated_normal(key, -4.0, 4.0, (BLOCKS, D, 3 * D), jnp.float32) * D ** (-0.5)
    return weights.astype(jnp.bfloat16)


def gaussian(stream_key, shape, deviation, limit, dtype=jnp.bfloat16):
    return jnp.clip(deviation * jax.random.normal(stream_key, shape, jnp.float32), -limit, limit).astype(dtype)


def setup_inputs(seed: int = 0) -> dict:
    key_of = jax.random.split(jax.random.key(seed), 4)
    video = draw_video(jax.random.fold_in(key_of[3], 71), 0)
    w_triple = draw_w_triple(jax.random.fold_in(key_of[3], 71), 0)
    w_out = gaussian(key_of[2], (BLOCKS, D, D), D ** -0.5, 0.1875)
    return {"video": video, "w_triple": w_triple, "w_out": w_out}


eps = 1e-06
time_forms = ('sabhe,tabhe->abhst', 'abhst,tabhe->sabhe')
height_forms = ('asbhe,atbhe->abhst', 'abhst,atbhe->asbhe')

def attend_full(triple, forms):
    lead = triple.shape[:-1]
    pieces = triple.reshape(lead + (3, HEADS, HEAD)).astype(jnp.float32)
    query = pieces[..., 0, :, :]
    keys = pieces[..., 1, :, :]
    values = pieces[..., 2, :, :]
    scores = jnp.einsum(forms[0], query, keys) * (1.0 / HEAD ** 0.5)
    top = lax.optimization_barrier(jnp.max(scores, axis=-1, keepdims=True))
    expo = jnp.exp(scores - top)
    probs = (expo / lax.optimization_barrier(jnp.sum(expo, axis=-1, keepdims=True))).astype(jnp.bfloat16)
    context = jnp.einsum(forms[1], probs.astype(jnp.float32), values)
    return context.astype(jnp.bfloat16).reshape(lead + (D,))

def reference(video, w_triple, w_out):
    state = video
    for layer in range(BLOCKS):
        forms = time_forms if layer % 2 == 0 else height_forms
        floats = state.astype(jnp.float32)
        normed = (floats * lax.rsqrt(lax.optimization_barrier(jnp.mean(floats * floats, axis=-1, keepdims=True)) + eps)).astype(jnp.bfloat16)
        triple = jnp.dot(normed.reshape(-1, D), w_triple[layer], preferred_element_type=jnp.float32)
        triple = triple.astype(jnp.bfloat16).reshape(state.shape[:-1] + (3 * D,))
        context = attend_full(triple, forms)
        update = jnp.dot(context.reshape(-1, D), w_out[layer], preferred_element_type=jnp.float32)
        state = (floats + update.reshape(floats.shape)).astype(jnp.bfloat16)
    return state
```

```python
import functools
import math

import jax
import jax.numpy as jnp
from jax import lax
from jax.experimental import pallas as pl
from jax.experimental.pallas import tpu as pltpu
from jax.sharding import PartitionSpec as P

D = 1024
HEADS = 16
HEAD = 64
EPS = 1e-06
PAIRS = HEADS // 2
SCALE = math.log2(math.e) / math.sqrt(HEAD)
BF = jnp.bfloat16
F32 = jnp.float32

LINE = 128
GROUP = 256


def relayout_kernel(perm_ref, x_ref, o_ref):
    x = x_ref[...].reshape(GROUP, D)
    y = jnp.dot(perm_ref[...], x, preferred_element_type=F32).astype(BF)
    o_ref[...] = y.reshape(o_ref.shape)


def permutation(rows, columns):
    return (rows[:, None] == columns[None, :]).astype(BF)


def to_columns(video):
    o = jnp.arange(GROUP)
    want = (o % 4) * 64 + ((o // 4) % 2) * 32 + o // 8
    perm = permutation(want, o)
    return pl.pallas_call(
        relayout_kernel,
        grid=(4,),
        in_specs=[
            pl.BlockSpec((GROUP, GROUP), lambda t: (0, 0)),
            pl.BlockSpec((4, 2, 32, D), lambda t: (0, t, 0, 0)),
        ],
        out_specs=pl.BlockSpec((32, None, 8, D), lambda t: (0, t, 0, 0)),
        out_shape=jax.ShapeDtypeStruct((32, 4, 8, D), BF),
        name="to_columns",
    )(perm, video)


def to_tokens(columns):
    o = jnp.arange(GROUP)
    want = (o % 32) * 8 + o // 32
    perm = permutation(want, o)
    return pl.pallas_call(
        relayout_kernel,
        grid=(4,),
        in_specs=[
            pl.BlockSpec((GROUP, GROUP), lambda j: (0, 0)),
            pl.BlockSpec((32, None, 8, D), lambda j: (0, j, 0, 0)),
        ],
        out_specs=pl.BlockSpec((None, 8, 32, D), lambda j: (j, 0, 0, 0)),
        out_shape=jax.ShapeDtypeStruct((4, 8, 32, D), BF),
        name="to_tokens",
    )(perm, columns)


def load_tokens(perm, pieces, xp_ref, normed_ref, at):
    x = jnp.concatenate(pieces, axis=0) if len(pieces) > 1 else pieces[0]
    x = jnp.dot(perm, x, preferred_element_type=F32)
    xp_ref[pl.ds(at, GROUP), :] = x.astype(BF)
    power = jnp.mean(x * x, axis=-1, keepdims=True)
    normed_ref[pl.ds(at, GROUP), :] = (x * lax.rsqrt(power + EPS)).astype(BF)


def project(normed_ref, w_ref, qkv_ref, step=512):
    @pl.loop(0, 3 * D // step)
    def _(n):
        at = pl.multiple_of(n * step, step)
        acc = jnp.dot(normed_ref[...], w_ref[:, pl.ds(at, step)], preferred_element_type=F32)
        qkv_ref[:, pl.ds(at, step)] = acc.astype(BF)


def attend(qkv_ref, ctx_ref, masked):
    tokens = qkv_ref.shape[0]
    low = (lax.broadcasted_iota(jnp.int32, (LINE, LINE), 1) < HEAD).astype(F32)
    low, high = low.astype(BF), (1.0 - low).astype(BF)
    if masked:
        a = lax.broadcasted_iota(jnp.int32, (2 * LINE, LINE), 0) % LINE // 32
        b = lax.broadcasted_iota(jnp.int32, (2 * LINE, LINE), 1) // 32
        same = a == b

    @pl.loop(0, tokens // LINE)
    def _(i):
        rows = pl.ds(pl.multiple_of(i * LINE, LINE), LINE)
        for p in range(PAIRS):
            q = qkv_ref[rows, p * 128 : p * 128 + 128]
            k = qkv_ref[rows, D + p * 128 : D + p * 128 + 128]
            v = qkv_ref[rows, 2 * D + p * 128 : 2 * D + p * 128 + 128]
            q = jnp.concatenate([q * low, q * high], axis=0)
            s = lax.dot_general(q, k, (((1,), (1,)), ((), ())), preferred_element_type=F32)
            if masked:
                s = jnp.where(same, s, -1e30)
            top = jnp.max(s, axis=-1, keepdims=True)
            e = jnp.exp2((s - top) * SCALE).astype(BF)
            e = jnp.concatenate([e[:LINE], e[LINE:]], axis=1)
            v = jnp.concatenate(
                [
                    jnp.concatenate([v * low, low], axis=1),
                    jnp.concatenate([v * high, high], axis=1),
                ],
                axis=0,
            )
            o = jnp.dot(e, v, preferred_element_type=F32)
            ctx_ref[rows, p * 128 : p * 128 + 128] = (o[:, :128] / o[:, 128:]).astype(BF)


def update(xp_ref, ctx_ref, wo_ref, y_ref, step=512):
    for at in range(0, D, step):
        acc = jnp.dot(ctx_ref[...], wo_ref[:, at : at + step], preferred_element_type=F32)
        y_ref[:, at : at + step] = (xp_ref[:, at : at + step].astype(F32) + acc).astype(BF)


def time_kernel(perm_ref, x_ref, w_ref, wo_ref, *refs):
    outs, (xp_ref, normed_ref, qkv_ref, ctx_ref) = refs[:4], refs[4:]
    perm = perm_ref[...]
    groups = x_ref.shape[1]
    for t in range(groups):
        load_tokens(perm, [x_ref[:, t].reshape(GROUP, D)], xp_ref, normed_ref, t * GROUP)
    project(normed_ref, w_ref, qkv_ref)
    attend(qkv_ref, ctx_ref, False)
    update(xp_ref, ctx_ref, wo_ref, normed_ref)
    for r in range(2 * groups):
        for s in range(4):
            at = (r * 4 + s) * 32
            outs[s][r] = normed_ref[at : at + 32, :]


def scratch(tokens):
    return [
        pltpu.VMEM((tokens, D), BF),
        pltpu.VMEM((tokens, D), BF),
        pltpu.VMEM((tokens, 3 * D), BF),
        pltpu.VMEM((tokens, D), BF),
    ]


def block_cost(tokens):
    return pl.CostEstimate(
        flops=2 * tokens * D * D * 4 + 4 * tokens * 128 * D,
        bytes_accessed=8 * D * D + 4 * tokens * D,
        transcendentals=tokens * 128 * HEADS,
    )


def time_block(perm, lines, w_triple, w_out, k, groups):
    tokens = groups * GROUP
    shape = jax.ShapeDtypeStruct((2 * groups, 32, D), BF)
    return pl.pallas_call(
        time_kernel,
        grid=(1,),
        in_specs=[
            pl.BlockSpec((GROUP, GROUP), lambda i: (0, 0)),
            pl.BlockSpec((32, groups, 8, D), lambda i: (0, k, 0, 0)),
            pl.BlockSpec((None, D, 3 * D), lambda i: (0, 0, 0)),
            pl.BlockSpec((None, D, D), lambda i: (0, 0, 0)),
        ],
        out_specs=[pl.BlockSpec((2 * groups, 32, D), lambda i: (0, 0, 0))] * 4,
        out_shape=[shape] * 4,
        scratch_shapes=scratch(tokens),
        cost_estimate=block_cost(tokens),
        compiler_params=pltpu.CompilerParams(vmem_limit_bytes=48 * 2**20),
        name=f"time_block_{k}",
    )(perm, lines, w_triple, w_out)


def height_kernel(n, perm_ref, *refs):
    pieces, (w_ref, wo_ref, y_ref), (xp_ref, normed_ref, qkv_ref, ctx_ref) = (
        refs[:n],
        refs[n : n + 3],
        refs[n + 3 :],
    )
    perm = perm_ref[...]
    groups = y_ref.shape[0] // 8
    for t in range(groups):
        parts = [
            piece[r, t * 8 : t * 8 + 8, :] for piece in pieces for r in range(piece.shape[0])
        ]
        load_tokens(perm, parts, xp_ref, normed_ref, t * GROUP)
    project(normed_ref, w_ref, qkv_ref)
    attend(qkv_ref, ctx_ref, True)
    update(xp_ref, ctx_ref, wo_ref, normed_ref)
    y_ref[...] = normed_ref[...].reshape(y_ref.shape)


def height_block(perm, pieces, w_triple, w_out, k, groups):
    tokens = groups * GROUP
    rows = pieces[0].shape[0]
    return pl.pallas_call(
        functools.partial(height_kernel, len(pieces)),
        grid=(1,),
        in_specs=[pl.BlockSpec((GROUP, GROUP), lambda i: (0, 0))]
        + [pl.BlockSpec((rows, 8 * groups, D), lambda i: (0, k, 0))] * len(pieces)
        + [
            pl.BlockSpec((None, D, 3 * D), lambda i: (1, 0, 0)),
            pl.BlockSpec((None, D, D), lambda i: (1, 0, 0)),
        ],
        out_specs=pl.BlockSpec((8 * groups, 32, D), lambda i: (0, 0, 0)),
        out_shape=jax.ShapeDtypeStruct((8 * groups, 32, D), BF),
        scratch_shapes=scratch(tokens),
        cost_estimate=block_cost(tokens),
        compiler_params=pltpu.CompilerParams(vmem_limit_bytes=48 * 2**20),
        name=f"height_block_{k}",
    )(perm, *pieces, w_triple, w_out)


CHUNKS0 = 2
CHUNKS1 = 1


def on_device(video, w_triple, w_out):
    g = lax.axis_index("grp")
    o = jnp.arange(GROUP)
    want = (o % 32) * 8 + (o // 128) * 4 + (((o // 32) % 4) ^ g)
    perm0 = permutation(want, o)
    rows = 8 // CHUNKS0
    m, rg, r = o // 32, (o // 8) % 4, o % 8
    want = (((r // rows) * 4 + (rg ^ g)) * rows + r % rows) * 8 + m
    perm1 = permutation(want, o)

    lines = lax.all_to_all(to_columns(video), "mem", split_axis=0, concat_axis=0, tiled=True)
    pieces = []
    for k in range(CHUNKS0):
        outs = time_block(perm0, lines, w_triple, w_out, k, 4 // CHUNKS0)
        pieces.append(outs[0])
        for s in range(1, 4):
            pieces.append(lax.ppermute(outs[s], "grp", [(i, i ^ s) for i in range(4)]))
    done = [
        height_block(perm1, pieces, w_triple, w_out, k, 4 // CHUNKS1) for k in range(CHUNKS1)
    ]
    done = jnp.concatenate(done, axis=0) if CHUNKS1 > 1 else done[0]
    done = lax.all_to_all(
        done.reshape(128, 8, D), ("mem", "grp"), split_axis=0, concat_axis=0, tiled=True
    )
    return to_tokens(done.reshape(32, 4, 8, D))


def solution(mesh):
    return jax.shard_map(
        on_device,
        mesh=mesh,
        in_specs=(P("mem", "grp", None, None), P(), P()),
        out_specs=P("mem", "grp", None, None),
        check_vma=False,
    )
```

```python
import functools
import math

import jax
import jax.numpy as jnp
from jax import lax
from jax.experimental import pallas as pl
from jax.experimental.pallas import tpu as pltpu
from jax.sharding import PartitionSpec as P

D = 1024
HEADS = 16
HEAD = 64
EPS = 1e-06
PAIRS = HEADS // 2
SCALE = math.log2(math.e) / math.sqrt(HEAD)
BF = jnp.bfloat16
F32 = jnp.float32

LINE = 128
GROUP = 256
LIMIT = 50 * 2**20
STEP = 512


def permutation(rows, columns):
    return (rows[:, None] == columns[None, :]).astype(BF)


def reorder(source, x):
    row = lax.broadcasted_iota(jnp.int32, (GROUP, GROUP), 0)
    column = lax.broadcasted_iota(jnp.int32, (GROUP, GROUP), 1)
    perm = (source(row) == column).astype(F32).astype(BF)
    return jnp.dot(perm, x, preferred_element_type=F32).astype(BF)


def to_columns_kernel(x_ref, o_ref, held_ref, sems):
    copies = [
        pltpu.make_async_copy(x_ref.at[:, pl.ds(2 * t, 2)], held_ref.at[t], sems.at[t])
        for t in range(4)
    ]
    for copy in copies:
        copy.start()
    for t, copy in enumerate(copies):
        copy.wait()
        y = reorder(
            lambda o: (o % 4) * 64 + ((o // 4) % 2) * 32 + o // 8, held_ref[t].reshape(GROUP, D)
        )
        o_ref[:, t] = y.reshape(32, 8, D)


def to_columns(video):
    return pl.pallas_call(
        to_columns_kernel,
        in_specs=[pl.BlockSpec(memory_space=pltpu.HBM)],
        out_specs=pl.BlockSpec(memory_space=pltpu.VMEM),
        out_shape=jax.ShapeDtypeStruct((32, 4, 8, D), BF),
        scratch_shapes=[pltpu.VMEM((4, 4, 2, 32, D), BF), pltpu.SemaphoreType.DMA((4,))],
        compiler_params=pltpu.CompilerParams(vmem_limit_bytes=60 * 2**20),
        name="to_columns",
    )(video)


def to_tokens_kernel(x_ref, o_ref, held_ref, sems):
    copies = []
    for j in range(4):
        y = reorder(lambda o: (o % 32) * 8 + o // 32, x_ref[:, j].reshape(GROUP, D))
        held_ref[j] = y.reshape(8, 32, D)
        copies.append(pltpu.make_async_copy(held_ref.at[j], o_ref.at[j], sems.at[j]))
        copies[-1].start()
    for copy in copies:
        copy.wait()


def to_tokens(columns):
    return pl.pallas_call(
        to_tokens_kernel,
        in_specs=[pl.BlockSpec(memory_space=pltpu.VMEM)],
        out_specs=pl.BlockSpec(memory_space=pltpu.HBM),
        out_shape=jax.ShapeDtypeStruct((4, 8, 32, D), BF),
        scratch_shapes=[pltpu.VMEM((4, 8, 32, D), BF), pltpu.SemaphoreType.DMA((4,))],
        compiler_params=pltpu.CompilerParams(vmem_limit_bytes=LIMIT),
        name="to_tokens",
    )(columns)


def weight_copies(w_ref, wo_ref, w_held, wo_held, sems, layer):
    copies = [
        pltpu.make_async_copy(
            w_ref.at[layer, :, pl.ds(i * STEP, STEP)],
            w_held.at[:, pl.ds(i * STEP, STEP)],
            sems.at[i],
        )
        for i in range(3 * D // STEP)
    ]
    copies.append(pltpu.make_async_copy(wo_ref.at[layer], wo_held, sems.at[3 * D // STEP]))
    return copies


def load_tokens(perm, pieces, xp_ref, normed_ref, at):
    x = jnp.concatenate(pieces, axis=0) if len(pieces) > 1 else pieces[0]
    x = jnp.dot(perm, x, preferred_element_type=F32)
    xp_ref[pl.ds(at, GROUP), :] = x.astype(BF)
    power = jnp.mean(x * x, axis=-1, keepdims=True)
    normed_ref[pl.ds(at, GROUP), :] = (x * lax.rsqrt(power + EPS)).astype(BF)


def project(normed_ref, w_ref, qkv_ref, copies):
    for i, copy in enumerate(copies):
        copy.wait()
        at = i * STEP
        acc = jnp.dot(normed_ref[...], w_ref[:, at : at + STEP], preferred_element_type=F32)
        qkv_ref[:, at : at + STEP] = acc.astype(BF)


def attend(qkv_ref, ctx_ref, masked):
    tokens = qkv_ref.shape[0]
    low = (lax.broadcasted_iota(jnp.int32, (LINE, LINE), 1) < HEAD).astype(F32)
    low, high = low.astype(BF), (1.0 - low).astype(BF)
    if masked:
        a = lax.broadcasted_iota(jnp.int32, (2 * LINE, LINE), 0) % LINE // 32
        b = lax.broadcasted_iota(jnp.int32, (2 * LINE, LINE), 1) // 32
        same = a == b

    @pl.loop(0, tokens // LINE)
    def _(i):
        rows = pl.ds(pl.multiple_of(i * LINE, LINE), LINE)
        for p in range(PAIRS):
            q = qkv_ref[rows, p * 128 : p * 128 + 128]
            k = qkv_ref[rows, D + p * 128 : D + p * 128 + 128]
            v = qkv_ref[rows, 2 * D + p * 128 : 2 * D + p * 128 + 128]
            q = jnp.concatenate([q * low, q * high], axis=0)
            s = lax.dot_general(q, k, (((1,), (1,)), ((), ())), preferred_element_type=F32)
            if masked:
                s = jnp.where(same, s, -1e30)
            top = jnp.max(s, axis=-1, keepdims=True)
            e = jnp.exp2((s - top) * SCALE).astype(BF)
            e = jnp.concatenate([e[:LINE], e[LINE:]], axis=1)
            v = jnp.concatenate(
                [
                    jnp.concatenate([v * low, low], axis=1),
                    jnp.concatenate([v * high, high], axis=1),
                ],
                axis=0,
            )
            o = jnp.dot(e, v, preferred_element_type=F32)
            ctx_ref[rows, p * 128 : p * 128 + 128] = (o[:, :128] / o[:, 128:]).astype(BF)


def update(xp_ref, ctx_ref, wo_ref, y_ref, step=512):
    for at in range(0, D, step):
        acc = jnp.dot(ctx_ref[...], wo_ref[:, at : at + step], preferred_element_type=F32)
        y_ref[:, at : at + step] = (xp_ref[:, at : at + step].astype(F32) + acc).astype(BF)


def run_block(loads, w_refs, work, layer, masked):
    w_ref, wo_ref = w_refs
    xp_ref, normed_ref, qkv_ref, ctx_ref, w_held, wo_held, sems = work
    copies = weight_copies(w_ref, wo_ref, w_held, wo_held, sems, layer)
    for copy in copies:
        copy.start()
    loads(xp_ref, normed_ref)
    project(normed_ref, w_held, qkv_ref, copies[:-1])
    attend(qkv_ref, ctx_ref, masked)
    copies[-1].wait()
    update(xp_ref, ctx_ref, wo_held, normed_ref)
    return normed_ref


def scratch(tokens):
    return [
        pltpu.VMEM((tokens, D), BF),
        pltpu.VMEM((tokens, D), BF),
        pltpu.VMEM((tokens, 3 * D), BF),
        pltpu.VMEM((tokens, D), BF),
        pltpu.VMEM((D, 3 * D), BF),
        pltpu.VMEM((D, D), BF),
        pltpu.SemaphoreType.DMA((3 * D // STEP + 1,)),
    ]


def block_cost(tokens):
    return pl.CostEstimate(
        flops=2 * tokens * D * D * 4 + 4 * tokens * 128 * D,
        bytes_accessed=8 * D * D + 4 * tokens * D,
        transcendentals=tokens * 128 * HEADS,
    )


def time_kernel(perm_ref, x_ref, *refs, k, groups, halves):
    w_refs, outs, work = refs[:2], refs[2 : 2 + 4 * halves], refs[2 + 4 * halves :]

    def loads(xp_ref, normed_ref):
        perm = perm_ref[...]
        for t in range(groups):
            x = x_ref[:, k * groups + t].reshape(GROUP, D)
            load_tokens(perm, [x], xp_ref, normed_ref, t * GROUP)

    y_ref = run_block(loads, w_refs, work, 0, False)
    span = 32 // halves
    for r in range(2 * groups):
        for s in range(4):
            for h in range(halves):
                at = (r * 4 + s) * 32 + h * span
                outs[s * halves + h][r] = y_ref[at : at + span, :]


def time_block(perm, lines, w_triple, w_out, k, groups, halves):
    tokens = groups * GROUP
    return pl.pallas_call(
        functools.partial(time_kernel, k=k, groups=groups, halves=halves),
        in_specs=[pl.BlockSpec(memory_space=pltpu.VMEM)] * 2
        + [pl.BlockSpec(memory_space=pltpu.HBM)] * 2,
        out_specs=[pl.BlockSpec(memory_space=pltpu.VMEM)] * (4 * halves),
        out_shape=[jax.ShapeDtypeStruct((2 * groups, 32 // halves, D), BF)] * (4 * halves),
        scratch_shapes=scratch(tokens),
        cost_estimate=block_cost(tokens),
        compiler_params=pltpu.CompilerParams(vmem_limit_bytes=LIMIT),
        name=f"time_block_{k}",
    )(perm, lines, w_triple, w_out)


def height_kernel(perm_ref, *refs, offsets, groups):
    n = len(offsets)
    pieces, w_refs, y_ref, work = refs[:n], refs[n : n + 2], refs[n + 2], refs[n + 3 :]

    def loads(xp_ref, normed_ref):
        perm = perm_ref[...]
        for t in range(groups):
            parts = [
                piece[r, at + t * 8 : at + t * 8 + 8, :]
                for piece, at in zip(pieces, offsets)
                for r in range(piece.shape[0])
            ]
            load_tokens(perm, parts, xp_ref, normed_ref, t * GROUP)

    out = run_block(loads, w_refs, work, 1, True)
    y_ref[...] = out[...].reshape(y_ref.shape)


def height_block(perm, pieces, offsets, w_triple, w_out, k, groups):
    tokens = groups * GROUP
    return pl.pallas_call(
        functools.partial(height_kernel, offsets=offsets, groups=groups),
        in_specs=[pl.BlockSpec(memory_space=pltpu.VMEM)] * (len(pieces) + 1)
        + [pl.BlockSpec(memory_space=pltpu.HBM)] * 2,
        out_specs=pl.BlockSpec(memory_space=pltpu.VMEM),
        out_shape=jax.ShapeDtypeStruct((8 * groups, 32, D), BF),
        scratch_shapes=scratch(tokens),
        cost_estimate=block_cost(tokens),
        compiler_params=pltpu.CompilerParams(vmem_limit_bytes=LIMIT),
        name=f"height_block_{k}",
    )(perm, *pieces, w_triple, w_out)


CHUNKS0 = 2
CHUNKS1 = 1
HALVES = (1, 1)


def on_device(video, w_triple, w_out):
    g = lax.axis_index("grp")
    o = jnp.arange(GROUP)
    want = (o % 32) * 8 + (o // 128) * 4 + (((o // 32) % 4) ^ g)
    perm0 = permutation(want, o)
    rows = 8 // CHUNKS0
    m, rg, r = o // 32, (o // 8) % 4, o % 8
    want = (((r // rows) * 4 + (rg ^ g)) * rows + r % rows) * 8 + m
    perm1 = permutation(want, o)

    lines = lax.all_to_all(to_columns(video), "mem", split_axis=0, concat_axis=0, tiled=True)
    pieces = []
    for k in range(CHUNKS0):
        halves = HALVES[k]
        outs = time_block(perm0, lines, w_triple, w_out, k, 4 // CHUNKS0, halves)
        for s in range(4):
            pairs = [(i, i ^ s) for i in range(4)]
            trade = (lambda x: lax.ppermute(x, "grp", pairs)) if s else (lambda x: x)
            pieces.append([trade(outs[s * halves + h]) for h in range(halves)])
    done = []
    for k in range(CHUNKS1):
        at = k * 32 // CHUNKS1
        chosen, offsets = [], []
        for piece in pieces:
            span = piece[0].shape[1]
            chosen.append(piece[at // span])
            offsets.append(at % span)
        done.append(
            height_block(perm1, chosen, tuple(offsets), w_triple, w_out, k, 4 // CHUNKS1)
        )
    done = jnp.concatenate(done, axis=0) if CHUNKS1 > 1 else done[0]
    done = lax.all_to_all(
        done.reshape(128, 8, D), ("mem", "grp"), split_axis=0, concat_axis=0, tiled=True
    )
    return to_tokens(done.reshape(32, 4, 8, D))


def solution(mesh):
    return jax.shard_map(
        on_device,
        mesh=mesh,
        in_specs=(P("mem", "grp", None, None), P(), P()),
        out_specs=P("mem", "grp", None, None),
        check_vma=False,
    )
```

```python
import functools
import math

import jax
import jax.numpy as jnp
from jax import lax
from jax.experimental import pallas as pl
from jax.experimental.pallas import tpu as pltpu
from jax.sharding import PartitionSpec as P

D = 1024
HEADS = 16
HEAD = 64
EPS = 1e-06
PAIRS = HEADS // 2
SCALE = math.log2(math.e) / math.sqrt(HEAD)
BF = jnp.bfloat16
F32 = jnp.float32

LINE = 128
GROUP = 256
LIMIT = 50 * 2**20
STEP = 512


def permutation(rows, columns):
    return (rows[:, None] == columns[None, :]).astype(BF)


def reorder(source, x):
    row = lax.broadcasted_iota(jnp.int32, (GROUP, GROUP), 0)
    column = lax.broadcasted_iota(jnp.int32, (GROUP, GROUP), 1)
    perm = (source(row) == column).astype(F32).astype(BF)
    return jnp.dot(perm, x, preferred_element_type=F32).astype(BF)


def to_columns_kernel(x_ref, o_ref, held_ref, out_ref, sems, out_sems):
    copies = [
        pltpu.make_async_copy(x_ref.at[:, pl.ds(2 * t, 2)], held_ref.at[t], sems.at[t])
        for t in range(4)
    ]
    for copy in copies:
        copy.start()
    outs = []
    for t, copy in enumerate(copies):
        copy.wait()
        y = reorder(
            lambda o: (o % 4) * 64 + ((o // 4) % 2) * 32 + o // 8, held_ref[t].reshape(GROUP, D)
        )
        out_ref[t] = y.reshape(32, 8, D)
        outs.append(pltpu.make_async_copy(out_ref.at[t], o_ref.at[:, t], out_sems.at[t]))
        outs[-1].start()
    for copy in outs:
        copy.wait()


def to_columns(video):
    return pl.pallas_call(
        to_columns_kernel,
        in_specs=[pl.BlockSpec(memory_space=pltpu.HBM)],
        out_specs=pl.BlockSpec(memory_space=pltpu.HBM),
        out_shape=jax.ShapeDtypeStruct((32, 4, 8, D), BF),
        scratch_shapes=[
            pltpu.VMEM((4, 4, 2, 32, D), BF),
            pltpu.VMEM((4, 32, 8, D), BF),
            pltpu.SemaphoreType.DMA((4,)),
            pltpu.SemaphoreType.DMA((4,)),
        ],
        compiler_params=pltpu.CompilerParams(vmem_limit_bytes=60 * 2**20),
        name="to_columns",
    )(video)


def to_tokens_kernel(x_ref, o_ref, held_ref, sems):
    copies = []
    for j in range(4):
        y = reorder(lambda o: (o % 32) * 8 + o // 32, x_ref[:, j].reshape(GROUP, D))
        held_ref[j] = y.reshape(8, 32, D)
        copies.append(pltpu.make_async_copy(held_ref.at[j], o_ref.at[j], sems.at[j]))
        copies[-1].start()
    for copy in copies:
        copy.wait()


def to_tokens(columns):
    return pl.pallas_call(
        to_tokens_kernel,
        in_specs=[pl.BlockSpec(memory_space=pltpu.VMEM)],
        out_specs=pl.BlockSpec(memory_space=pltpu.HBM),
        out_shape=jax.ShapeDtypeStruct((4, 8, 32, D), BF),
        scratch_shapes=[pltpu.VMEM((4, 8, 32, D), BF), pltpu.SemaphoreType.DMA((4,))],
        compiler_params=pltpu.CompilerParams(vmem_limit_bytes=LIMIT),
        name="to_tokens",
    )(columns)


def weight_copy(w_ref, w_held, sems, layer, i):
    columns = pl.ds(pl.multiple_of(i * STEP, STEP), STEP)
    return pltpu.make_async_copy(
        w_ref.at[layer, :, columns], w_held.at[:, columns], sems.at[i]
    )


def load_tokens(perm, x, xp_ref, normed_ref, at):
    x = jnp.dot(perm, x, preferred_element_type=F32)
    rows = slice(at, at + x.shape[0])
    xp_ref[rows, :] = x.astype(BF)
    power = jnp.mean(x * x, axis=-1, keepdims=True)
    normed_ref[rows, :] = (x * lax.rsqrt(power + EPS)).astype(BF)


def project(normed_ref, w_held, qkv_ref, wait):
    for i in range(3 * D // STEP):
        wait(i)
        columns = slice(i * STEP, i * STEP + STEP)
        acc = jnp.dot(normed_ref[...], w_held[:, columns], preferred_element_type=F32)
        qkv_ref[:, columns] = acc.astype(BF)


def masks():
    low = (lax.broadcasted_iota(jnp.int32, (LINE, LINE), 1) < HEAD).astype(F32)
    return low.astype(BF), (1.0 - low).astype(BF)


def attend(q, k, v, low, high, same):
    q = jnp.concatenate([q * low, q * high], axis=0)
    s = lax.dot_general(q, k, (((1,), (1,)), ((), ())), preferred_element_type=F32)
    if same is not None:
        s = jnp.where(same, s, -1e30)
    top = jnp.max(s, axis=-1, keepdims=True)
    e = jnp.exp2((s - top) * SCALE).astype(BF)
    e = jnp.concatenate([e[:LINE], e[LINE:]], axis=1)
    v = jnp.concatenate(
        [
            jnp.concatenate([v * low, low], axis=1),
            jnp.concatenate([v * high, high], axis=1),
        ],
        axis=0,
    )
    o = jnp.dot(e, v, preferred_element_type=F32)
    return (o[:, :LINE] / o[:, LINE:]).astype(BF)


def start_weights(w_ref, w_held, sems, layer):
    copies = [weight_copy(w_ref, w_held, sems, layer, i) for i in range(3 * D // STEP)]
    for copy in copies:
        copy.start()
    return lambda i: copies[i].wait()


def cost(tokens, matmuls, attends):
    return pl.CostEstimate(
        flops=2 * tokens * D * D * matmuls + 4 * attends * 128 * D,
        bytes_accessed=2 * matmuls * D * D,
        transcendentals=attends * 128 * HEADS,
    )


def call(kernel, vmem, hbm, outs, scratch, estimate, name):
    return pl.pallas_call(
        kernel,
        in_specs=[pl.BlockSpec(memory_space=pltpu.VMEM)] * len(vmem)
        + [pl.BlockSpec(memory_space=pltpu.HBM)] * len(hbm),
        out_specs=[pl.BlockSpec(memory_space=pltpu.VMEM)] * len(outs),
        out_shape=[jax.ShapeDtypeStruct(shape, BF) for shape in outs],
        scratch_shapes=[pltpu.VMEM(shape, BF) for shape in scratch]
        + [pltpu.SemaphoreType.DMA((3 * D // STEP + 1,))],
        compiler_params=pltpu.CompilerParams(vmem_limit_bytes=LIMIT),
        cost_estimate=estimate,
        name=name,
    )(*vmem, *hbm)


def time_kernel(perm_ref, x_ref, w_ref, wo_ref, *refs, k):
    outs, (xp_ref, normed_ref, qkv_ref, ctx_ref, w_held, wo_held, sems) = refs[:4], refs[4:]
    wait = start_weights(w_ref, w_held, sems, 0)
    last = pltpu.make_async_copy(wo_ref.at[0], wo_held, sems.at[3 * D // STEP])
    last.start()
    perm = perm_ref[...]
    for t in range(2):
        x = x_ref[:, 2 * k + t].reshape(GROUP, D)
        load_tokens(perm, x, xp_ref, normed_ref, t * GROUP)
    project(normed_ref, w_held, qkv_ref, wait)
    low, high = masks()
    for line in range(4):
        rows = slice(line * LINE, line * LINE + LINE)
        for p in range(PAIRS):
            at = p * 128
            q, k_, v = (qkv_ref[rows, part + at : part + at + 128] for part in (0, D, 2 * D))
            ctx_ref[rows, at : at + 128] = attend(q, k_, v, low, high, None)
    last.wait()
    for at in range(0, D, STEP):
        columns = slice(at, at + STEP)
        y = jnp.dot(ctx_ref[...], wo_held[:, columns], preferred_element_type=F32)
        y = (xp_ref[:, columns].astype(F32) + y).astype(BF)
        for r in range(4):
            for s in range(4):
                row = (r * 4 + s) * 32
                outs[s][r, :, columns] = y[row : row + 32]


def time_block(perm, lines, w_triple, w_out, k):
    tokens = 512
    return call(
        functools.partial(time_kernel, k=k),
        [perm, lines],
        [w_triple, w_out],
        [(4, 32, D)] * 4,
        [(tokens, D), (tokens, D), (tokens, 3 * D), (tokens, D), (D, 3 * D), (D, D)],
        cost(tokens, 4, tokens),
        f"time_block_{k}",
    )


def load_rows(pieces, xp_ref, normed_ref):
    o = lax.broadcasted_iota(jnp.int32, (LINE, LINE), 0)
    i = lax.broadcasted_iota(jnp.int32, (LINE, LINE), 1)
    perm = ((o % 16) * 8 + o // 16 == i).astype(F32).astype(BF)
    for n in range(4):
        x = [piece[r, n * 8 : n * 8 + 8, :] for piece in pieces for r in range(4)]
        load_tokens(perm, jnp.concatenate(x, axis=0), xp_ref, normed_ref, n * LINE)


def early_kernel(*refs):
    pieces, w_ref, qkv_ref, xp_ref = refs[:4], refs[4], refs[5], refs[6]
    normed_ref, w_held, sems = refs[7:]
    wait = start_weights(w_ref, w_held, sems, 1)
    load_rows(pieces, xp_ref, normed_ref)
    project(normed_ref, w_held, qkv_ref, wait)


def early(pieces, w_triple):
    tokens = 512
    return call(
        early_kernel,
        pieces,
        [w_triple],
        [(tokens, 3 * D), (tokens, D)],
        [(tokens, D), (D, 3 * D)],
        cost(tokens, 3, 0),
        "early",
    )


def height_kernel(*refs):
    perm_ref, qkv_a, xp_a, pieces, w_ref, wo_ref, y_ref = *refs[:3], refs[3:7], *refs[7:10]
    xp_b, normed_ref, qkv_b, ctx_ref, w_held, wo_held, sems = refs[10:]
    wait = start_weights(w_ref, w_held, sems, 1)
    last = pltpu.make_async_copy(wo_ref.at[1], wo_held, sems.at[3 * D // STEP])
    last.start()
    load_rows(pieces, xp_b, normed_ref)
    project(normed_ref, w_held, qkv_b, wait)
    low, high = masks()
    a = lax.broadcasted_iota(jnp.int32, (2 * LINE, LINE), 0) % 64 // 16
    b = lax.broadcasted_iota(jnp.int32, (2 * LINE, LINE), 1) % 64 // 16
    same = a == b

    @pl.loop(0, 8 // UNROLL)
    def _(n):
        for j in range(UNROLL):
            i = n * UNROLL + j
            rows = pl.ds(pl.multiple_of(i * 64, 64), 64)
            for p in range(PAIRS):
                q, k, v = (
                    jnp.concatenate(
                        [ref[rows, part * D + p * 128 : part * D + p * 128 + 128] for ref in (qkv_a, qkv_b)]
                    )
                    for part in range(3)
                )
                o = attend(q, k, v, low, high, same)
                for half in range(2):
                    at = (i // 2) * 256 + half * 128 + (i % 2) * 64
                    at = pl.ds(pl.multiple_of(at, 64), 64)
                    ctx_ref[at, p * 128 : p * 128 + 128] = o[half * 64 : half * 64 + 64]

    last.wait()
    for at in range(0, D, STEP):
        columns = slice(at, at + STEP)
        y = jnp.dot(ctx_ref[...], wo_held[:, columns], preferred_element_type=F32)
        for n in range(4):
            x = [xp[n * 128 : n * 128 + 128, columns] for xp in (xp_a, xp_b)]
            z = jnp.concatenate(x).astype(F32) + y[n * GROUP : n * GROUP + GROUP]
            z = jnp.dot(perm_ref[...], z.astype(BF), preferred_element_type=F32).astype(BF)
            y_ref[n * 8 : n * 8 + 8, :, columns] = z.reshape(8, 32, STEP)


def height_block(perm, qkv_a, xp_a, pieces, w_triple, w_out):
    tokens = 512
    return call(
        height_kernel,
        [perm, qkv_a, xp_a, *pieces],
        [w_triple, w_out],
        [(32, 32, D)],
        [(tokens, D), (tokens, D), (tokens, 3 * D), (2 * tokens, D), (D, 3 * D), (D, D)],
        cost(2 * tokens, 4, 2 * tokens),
        "height_block",
    )[0]


UNROLL = 4


def on_device(video, w_triple, w_out):
    g = lax.axis_index("grp")
    o = jnp.arange(GROUP)
    want = (o % 32) * 8 + (o // 128) * 4 + (((o // 32) % 4) ^ g)
    perm0 = permutation(want, o)
    want = ((o // 4) % 2) * 128 + (o // 32) * 16 + (((o // 8) % 4) ^ g) * 4 + o % 4
    perm1 = permutation(want, o)

    lines = lax.all_to_all(to_columns(video), "mem", split_axis=0, concat_axis=0, tiled=True)
    pieces = []
    for k in range(2):
        outs = time_block(perm0, lines, w_triple, w_out, k)
        pieces.append(
            [outs[0]]
            + [lax.ppermute(outs[s], "grp", [(i, i ^ s) for i in range(4)]) for s in range(1, 4)]
        )
    qkv, xp = early(pieces[0], w_triple)
    done = height_block(perm1, qkv, xp, pieces[1], w_triple, w_out)
    done = lax.all_to_all(
        done.reshape(128, 8, D), ("mem", "grp"), split_axis=0, concat_axis=0, tiled=True
    )
    return to_tokens(done.reshape(32, 4, 8, D))


def solution(mesh):
    return jax.shard_map(
        on_device,
        mesh=mesh,
        in_specs=(P("mem", "grp", None, None), P(), P()),
        out_specs=P("mem", "grp", None, None),
        check_vma=False,
    )
```

```python
import functools
import math

import jax
import jax.numpy as jnp
from jax import lax
from jax.experimental import pallas as pl
from jax.experimental.pallas import tpu as pltpu
from jax.sharding import PartitionSpec as P

D = 1024
HEADS = 16
HEAD = 64
EPS = 1e-06
PAIRS = HEADS // 2
SCALE = math.log2(math.e) / math.sqrt(HEAD)
BF = jnp.bfloat16
F32 = jnp.float32

LINE = 128
GROUP = 256
LIMIT = 50 * 2**20
EARLY_LIMIT = 44 * 2**20
HEIGHT_LIMIT = 36 * 2**20
STEP = 512


def permutation(rows, columns):
    return (rows[:, None] == columns[None, :]).astype(BF)


def reorder(source, x):
    row = lax.broadcasted_iota(jnp.int32, (GROUP, GROUP), 0)
    column = lax.broadcasted_iota(jnp.int32, (GROUP, GROUP), 1)
    perm = (source(row) == column).astype(F32).astype(BF)
    return jnp.dot(perm, x, preferred_element_type=F32).astype(BF)


def to_columns_kernel(x_ref, o_ref, held_ref, out_ref, sems, out_sems):
    copies = [
        pltpu.make_async_copy(x_ref.at[:, pl.ds(2 * t, 2)], held_ref.at[t], sems.at[t])
        for t in range(4)
    ]
    for copy in copies:
        copy.start()
    outs = []
    for t, copy in enumerate(copies):
        copy.wait()
        y = reorder(
            lambda o: (o % 4) * 64 + ((o // 4) % 2) * 32 + o // 8, held_ref[t].reshape(GROUP, D)
        )
        out_ref[t] = y.reshape(32, 8, D)
        outs.append(pltpu.make_async_copy(out_ref.at[t], o_ref.at[:, t], out_sems.at[t]))
        outs[-1].start()
    for copy in outs:
        copy.wait()


def to_columns(video):
    return pl.pallas_call(
        to_columns_kernel,
        in_specs=[pl.BlockSpec(memory_space=pltpu.HBM)],
        out_specs=pl.BlockSpec(memory_space=pltpu.HBM),
        out_shape=jax.ShapeDtypeStruct((32, 4, 8, D), BF),
        scratch_shapes=[
            pltpu.VMEM((4, 4, 2, 32, D), BF),
            pltpu.VMEM((4, 32, 8, D), BF),
            pltpu.SemaphoreType.DMA((4,)),
            pltpu.SemaphoreType.DMA((4,)),
        ],
        compiler_params=pltpu.CompilerParams(vmem_limit_bytes=60 * 2**20),
        name="to_columns",
    )(video)


def to_tokens_kernel(x_ref, o_ref, held_ref, sems):
    copies = []
    for j in range(4):
        y = reorder(lambda o: (o % 32) * 8 + o // 32, x_ref[:, j].reshape(GROUP, D))
        held_ref[j] = y.reshape(8, 32, D)
        copies.append(pltpu.make_async_copy(held_ref.at[j], o_ref.at[j], sems.at[j]))
        copies[-1].start()
    for copy in copies:
        copy.wait()


def to_tokens(columns):
    return pl.pallas_call(
        to_tokens_kernel,
        in_specs=[pl.BlockSpec(memory_space=pltpu.VMEM)],
        out_specs=pl.BlockSpec(memory_space=pltpu.HBM),
        out_shape=jax.ShapeDtypeStruct((4, 8, 32, D), BF),
        scratch_shapes=[pltpu.VMEM((4, 8, 32, D), BF), pltpu.SemaphoreType.DMA((4,))],
        compiler_params=pltpu.CompilerParams(vmem_limit_bytes=LIMIT),
        name="to_tokens",
    )(columns)


def weight_copy(w_ref, w_held, sems, layer, i):
    columns = pl.ds(pl.multiple_of(i * STEP, STEP), STEP)
    return pltpu.make_async_copy(
        w_ref.at[layer, :, columns], w_held.at[:, columns], sems.at[i]
    )


def load_tokens(perm, x, xp_ref, normed_ref, at):
    x = jnp.dot(perm, x, preferred_element_type=F32)
    rows = slice(at, at + x.shape[0])
    xp_ref[rows, :] = x.astype(BF)
    power = jnp.mean(x * x, axis=-1, keepdims=True)
    normed_ref[rows, :] = (x * lax.rsqrt(power + EPS)).astype(BF)


def project(normed_ref, w_held, qkv_ref, wait):
    for i in range(3 * D // STEP):
        wait(i)
        columns = slice(i * STEP, i * STEP + STEP)
        acc = jnp.dot(normed_ref[...], w_held[:, columns], preferred_element_type=F32)
        qkv_ref[:, columns] = acc.astype(BF)


def masks():
    low = (lax.broadcasted_iota(jnp.int32, (LINE, LINE), 1) < HEAD).astype(F32)
    return low.astype(BF), (1.0 - low).astype(BF)


def attend(q, k, v, low, high, same):
    q = jnp.concatenate([q * low, q * high], axis=0)
    s = lax.dot_general(q, k, (((1,), (1,)), ((), ())), preferred_element_type=F32)
    if same is not None:
        s = jnp.where(same, s, -1e30)
    top = jnp.max(s, axis=-1, keepdims=True)
    e = jnp.exp2((s - top) * SCALE).astype(BF)
    e = jnp.concatenate([e[:LINE], e[LINE:]], axis=1)
    v = jnp.concatenate(
        [
            jnp.concatenate([v * low, low], axis=1),
            jnp.concatenate([v * high, high], axis=1),
        ],
        axis=0,
    )
    o = jnp.dot(e, v, preferred_element_type=F32)
    return (o[:, :LINE] / o[:, LINE:]).astype(BF)


def start_weights(w_ref, w_held, sems, layer):
    copies = [weight_copy(w_ref, w_held, sems, layer, i) for i in range(3 * D // STEP)]
    for copy in copies:
        copy.start()
    return lambda i: copies[i].wait()


def cost(tokens, matmuls, attends):
    return pl.CostEstimate(
        flops=2 * tokens * D * D * matmuls + 4 * attends * 128 * D,
        bytes_accessed=2 * matmuls * D * D,
        transcendentals=attends * 128 * HEADS,
    )


def call(kernel, vmem, hbm, outs, scratch, estimate, name, limit=LIMIT):
    return pl.pallas_call(
        kernel,
        in_specs=[pl.BlockSpec(memory_space=pltpu.VMEM)] * len(vmem)
        + [pl.BlockSpec(memory_space=pltpu.HBM)] * len(hbm),
        out_specs=[pl.BlockSpec(memory_space=pltpu.VMEM)] * len(outs),
        out_shape=[jax.ShapeDtypeStruct(shape, BF) for shape in outs],
        scratch_shapes=[pltpu.VMEM(shape, BF) for shape in scratch]
        + [pltpu.SemaphoreType.DMA((3 * D // STEP + 1,))],
        compiler_params=pltpu.CompilerParams(vmem_limit_bytes=limit),
        cost_estimate=estimate,
        name=name,
    )(*vmem, *hbm)


def time_kernel(perm_ref, x_ref, w_ref, wo_ref, *refs, k):
    outs, (xp_ref, normed_ref, qkv_ref, ctx_ref, w_held, wo_held, sems) = refs[:4], refs[4:]
    wait = start_weights(w_ref, w_held, sems, 0)
    last = pltpu.make_async_copy(wo_ref.at[0], wo_held, sems.at[3 * D // STEP])
    last.start()
    perm = perm_ref[...]
    for t in range(2):
        x = x_ref[:, 2 * k + t].reshape(GROUP, D)
        load_tokens(perm, x, xp_ref, normed_ref, t * GROUP)
    project(normed_ref, w_held, qkv_ref, wait)
    low, high = masks()
    for line in range(4):
        rows = slice(line * LINE, line * LINE + LINE)
        for p in range(PAIRS):
            at = p * 128
            q, k_, v = (qkv_ref[rows, part + at : part + at + 128] for part in (0, D, 2 * D))
            ctx_ref[rows, at : at + 128] = attend(q, k_, v, low, high, None)
    last.wait()
    for at in range(0, D, STEP):
        columns = slice(at, at + STEP)
        y = jnp.dot(ctx_ref[...], wo_held[:, columns], preferred_element_type=F32)
        y = (xp_ref[:, columns].astype(F32) + y).astype(BF)
        for r in range(4):
            for s in range(4):
                row = (r * 4 + s) * 32
                outs[s][r, :, columns] = y[row : row + 32]


def time_block(perm, lines, w_triple, w_out, k):
    tokens = 512
    return call(
        functools.partial(time_kernel, k=k),
        [perm, lines],
        [w_triple, w_out],
        [(4, 32, D)] * 4,
        [(tokens, D), (tokens, D), (tokens, 3 * D), (tokens, D), (D, 3 * D), (D, D)],
        cost(tokens, 4, tokens),
        f"time_block_{k}",
    )


def load_rows(pieces, xp_ref, normed_ref, start):
    frame = 4 * len(pieces)
    span = 8 * frame
    o = lax.broadcasted_iota(jnp.int32, (span, span), 0)
    i = lax.broadcasted_iota(jnp.int32, (span, span), 1)
    perm = ((o % frame) * 8 + o // frame == i).astype(F32).astype(BF)
    for n in range(4):
        x = [piece[r, n * 8 : n * 8 + 8, :] for piece in pieces for r in range(4)]
        load_tokens(perm, jnp.concatenate(x, axis=0), xp_ref, normed_ref, start + n * span)


EARLY = 768
LATE = 256


def early_kernel(*refs):
    pieces, w_ref, qkv_ref, xp_ref = refs[:6], refs[6], refs[7], refs[8]
    normed_ref, w_held, sems = refs[9:]
    wait = start_weights(w_ref, w_held, sems, 1)
    load_rows(pieces[:4], xp_ref, normed_ref, 0)
    load_rows(pieces[4:], xp_ref, normed_ref, 512)
    project(normed_ref, w_held, qkv_ref, wait)


def early(pieces, w_triple):
    return call(
        early_kernel,
        pieces,
        [w_triple],
        [(EARLY, 3 * D), (EARLY, D)],
        [(EARLY, D), (D, 3 * D)],
        cost(EARLY, 3, 0),
        "early",
        EARLY_LIMIT,
    )


def height_kernel(*refs):
    perm_ref, qkv_a, xp_a, pieces, w_ref, wo_ref, y_ref = *refs[:3], refs[3:5], *refs[5:8]
    xp_b, normed_ref, qkv_b, ctx_ref, w_held, wo_held, sems = refs[8:]
    wait = start_weights(w_ref, w_held, sems, 1)
    last = pltpu.make_async_copy(wo_ref.at[1], wo_held, sems.at[3 * D // STEP])
    last.start()
    load_rows(pieces, xp_b, normed_ref, 0)
    project(normed_ref, w_held, qkv_b, wait)

    def run(early, late, i, columns):
        at = lambda base, size: pl.ds(pl.multiple_of(base + i * size, size), size)
        parts = [early[at(0, 64), columns], early[at(512, 32), columns], late[at(0, 32), columns]]
        return jnp.concatenate(parts, axis=0)

    def frame(shape, axis):
        t = lax.broadcasted_iota(jnp.int32, shape, axis) % LINE
        return jnp.where(t < 64, t // 16, t % 32 // 8)

    low, high = masks()
    same = frame((2 * LINE, LINE), 0) == frame((2 * LINE, LINE), 1)

    @pl.loop(0, 8 // UNROLL)
    def _(n):
        for j in range(UNROLL):
            i = n * UNROLL + j
            rows = pl.ds(pl.multiple_of(i * LINE, LINE), LINE)
            for at in range(0, D, 128):
                q, k, v = (
                    run(qkv_a, qkv_b, i, slice(part + at, part + at + 128))
                    for part in (0, D, 2 * D)
                )
                ctx_ref[rows, at : at + 128] = attend(q, k, v, low, high, same)

    last.wait()
    for at in range(0, D, STEP):
        columns = slice(at, at + STEP)
        y = jnp.dot(ctx_ref[...], wo_held[:, columns], preferred_element_type=F32)
        for n in range(4):
            x = jnp.concatenate([run(xp_a, xp_b, i, columns) for i in (2 * n, 2 * n + 1)], axis=0)
            z = x.astype(F32) + y[n * GROUP : n * GROUP + GROUP]
            z = jnp.dot(perm_ref[...], z.astype(BF), preferred_element_type=F32).astype(BF)
            y_ref[n * 8 : n * 8 + 8, :, columns] = z.reshape(8, 32, STEP)


def height_block(perm, qkv_a, xp_a, pieces, w_triple, w_out):
    return call(
        height_kernel,
        [perm, qkv_a, xp_a, *pieces],
        [w_triple, w_out],
        [(32, 32, D)],
        [(LATE, D), (LATE, D), (LATE, 3 * D), (1024, D), (D, 3 * D), (D, D)],
        cost(1024, 3, 1024),
        "height_block",
        HEIGHT_LIMIT,
    )[0]


UNROLL = 4


def on_device(video, w_triple, w_out):
    g = lax.axis_index("grp")
    o = jnp.arange(GROUP)
    want = (o % 32) * 8 + (o // 128) * 4 + (((o // 32) % 4) ^ g)
    perm0 = permutation(want, o)
    m, s, chunk, r = o // 32, ((o // 8) % 4) ^ g, (o // 4) % 2, o % 4
    first = (m % 4) * 16 + s * 4 + r
    second = 64 + (s // 2) * 32 + (m % 4) * 8 + (s % 2) * 4 + r
    perm1 = permutation((m // 4) * LINE + jnp.where(chunk == 0, first, second), o)

    lines = lax.all_to_all(to_columns(video), "mem", split_axis=0, concat_axis=0, tiled=True)
    pieces = []
    for k in range(2):
        outs = time_block(perm0, lines, w_triple, w_out, k)
        pieces.append(
            [outs[0]]
            + [lax.ppermute(outs[s], "grp", [(i, i ^ s) for i in range(4)]) for s in range(1, 4)]
        )
        if k == 0:
            lines, pieces[0][0] = lax.optimization_barrier((lines, pieces[0][0]))
    qkv, xp = early(pieces[0] + pieces[1][:2], w_triple)
    done = height_block(perm1, qkv, xp, pieces[1][2:], w_triple, w_out)
    done = lax.all_to_all(
        done.reshape(128, 8, D), ("mem", "grp"), split_axis=0, concat_axis=0, tiled=True
    )
    return to_tokens(done.reshape(32, 4, 8, D))


def solution(mesh):
    return jax.shard_map(
        on_device,
        mesh=mesh,
        in_specs=(P("mem", "grp", None, None), P(), P()),
        out_specs=P("mem", "grp", None, None),
        check_vma=False,
    )
```

```python
import functools
import math

import jax
import jax.numpy as jnp
from jax import lax
from jax.experimental import pallas as pl
from jax.experimental.pallas import tpu as pltpu
from jax.sharding import PartitionSpec as P

D = 1024
HEADS = 16
HEAD = 64
EPS = 1e-06
PAIRS = HEADS // 2
SCALE = math.log2(math.e) / math.sqrt(HEAD)
BF = jnp.bfloat16
F32 = jnp.float32

LINE = 128
GROUP = 256
LIMIT = 50 * 2**20
COLUMNS_LIMIT = 50 * 2**20
EARLY_LIMIT = 44 * 2**20
HEIGHT_LIMIT = 36 * 2**20
STEP = 512


def permutation(rows, columns):
    return (rows[:, None] == columns[None, :]).astype(BF)


def reorder(source, x):
    row = lax.broadcasted_iota(jnp.int32, (GROUP, GROUP), 0)
    column = lax.broadcasted_iota(jnp.int32, (GROUP, GROUP), 1)
    perm = (source(row) == column).astype(F32).astype(BF)
    return jnp.dot(perm, x, preferred_element_type=F32).astype(BF)


def to_columns_kernel(x_ref, o_ref, held_ref, sems):
    copies = [
        pltpu.make_async_copy(x_ref.at[:, pl.ds(2 * t, 2)], held_ref.at[t], sems.at[t])
        for t in range(4)
    ]
    for copy in copies:
        copy.start()
    for t, copy in enumerate(copies):
        copy.wait()
        y = reorder(
            lambda o: (o % 4) * 64 + ((o // 4) % 2) * 32 + o // 8, held_ref[t].reshape(GROUP, D)
        )
        o_ref[:, t] = y.reshape(32, 8, D)


def to_columns(video):
    return pl.pallas_call(
        to_columns_kernel,
        in_specs=[pl.BlockSpec(memory_space=pltpu.HBM)],
        out_specs=pl.BlockSpec(memory_space=pltpu.VMEM),
        out_shape=jax.ShapeDtypeStruct((32, 4, 8, D), BF),
        scratch_shapes=[
            pltpu.VMEM((4, 4, 2, 32, D), BF),
            pltpu.SemaphoreType.DMA((4,)),
        ],
        compiler_params=pltpu.CompilerParams(vmem_limit_bytes=COLUMNS_LIMIT),
        name="to_columns",
    )(video)


def to_tokens_kernel(x_ref, o_ref, held_ref, sems):
    copies = []
    for j in range(4):
        y = reorder(lambda o: (o % 32) * 8 + o // 32, x_ref[:, j].reshape(GROUP, D))
        held_ref[j] = y.reshape(8, 32, D)
        copies.append(pltpu.make_async_copy(held_ref.at[j], o_ref.at[j], sems.at[j]))
        copies[-1].start()
    for copy in copies:
        copy.wait()


def to_tokens(columns):
    return pl.pallas_call(
        to_tokens_kernel,
        in_specs=[pl.BlockSpec(memory_space=pltpu.VMEM)],
        out_specs=pl.BlockSpec(memory_space=pltpu.HBM),
        out_shape=jax.ShapeDtypeStruct((4, 8, 32, D), BF),
        scratch_shapes=[pltpu.VMEM((4, 8, 32, D), BF), pltpu.SemaphoreType.DMA((4,))],
        compiler_params=pltpu.CompilerParams(vmem_limit_bytes=LIMIT),
        name="to_tokens",
    )(columns)


def weight_copy(w_ref, w_held, sems, layer, i):
    columns = pl.ds(pl.multiple_of(i * STEP, STEP), STEP)
    return pltpu.make_async_copy(
        w_ref.at[layer, :, columns], w_held.at[:, columns], sems.at[i]
    )


def load_tokens(perm, x, xp_ref, normed_ref, at):
    x = jnp.dot(perm, x, preferred_element_type=F32)
    rows = slice(at, at + x.shape[0])
    xp_ref[rows, :] = x.astype(BF)
    power = jnp.mean(x * x, axis=-1, keepdims=True)
    normed_ref[rows, :] = (x * lax.rsqrt(power + EPS)).astype(BF)


def project(normed_ref, w_held, qkv_ref, wait):
    for i in range(3 * D // STEP):
        wait(i)
        columns = slice(i * STEP, i * STEP + STEP)
        acc = jnp.dot(normed_ref[...], w_held[:, columns], preferred_element_type=F32)
        qkv_ref[:, columns] = acc.astype(BF)


def masks():
    low = (lax.broadcasted_iota(jnp.int32, (LINE, LINE), 1) < HEAD).astype(F32)
    return low.astype(BF), (1.0 - low).astype(BF)


def attend(q, k, v, low, high, same):
    q = jnp.concatenate([q * low, q * high], axis=0)
    s = lax.dot_general(q, k, (((1,), (1,)), ((), ())), preferred_element_type=F32)
    if same is not None:
        s = jnp.where(same, s, -1e30)
    top = jnp.max(s, axis=-1, keepdims=True)
    e = jnp.exp2((s - top) * SCALE).astype(BF)
    e = jnp.concatenate([e[:LINE], e[LINE:]], axis=1)
    v = jnp.concatenate(
        [
            jnp.concatenate([v * low, low], axis=1),
            jnp.concatenate([v * high, high], axis=1),
        ],
        axis=0,
    )
    o = jnp.dot(e, v, preferred_element_type=F32)
    return (o[:, :LINE] / o[:, LINE:]).astype(BF)


def start_weights(w_ref, w_held, sems, layer):
    copies = [weight_copy(w_ref, w_held, sems, layer, i) for i in range(3 * D // STEP)]
    for copy in copies:
        copy.start()
    return lambda i: copies[i].wait()


def cost(tokens, matmuls, attends):
    return pl.CostEstimate(
        flops=2 * tokens * D * D * matmuls + 4 * attends * 128 * D,
        bytes_accessed=2 * matmuls * D * D,
        transcendentals=attends * 128 * HEADS,
    )


def call(kernel, vmem, hbm, outs, scratch, estimate, name, limit=LIMIT):
    return pl.pallas_call(
        kernel,
        in_specs=[pl.BlockSpec(memory_space=pltpu.VMEM)] * len(vmem)
        + [pl.BlockSpec(memory_space=pltpu.HBM)] * len(hbm),
        out_specs=[pl.BlockSpec(memory_space=pltpu.VMEM)] * len(outs),
        out_shape=[jax.ShapeDtypeStruct(shape, BF) for shape in outs],
        scratch_shapes=[pltpu.VMEM(shape, BF) for shape in scratch]
        + [pltpu.SemaphoreType.DMA((3 * D // STEP + 1,))],
        compiler_params=pltpu.CompilerParams(vmem_limit_bytes=limit),
        cost_estimate=estimate,
        name=name,
    )(*vmem, *hbm)


def time_kernel(perm_ref, x_ref, w_ref, wo_ref, *refs, k):
    outs, (xp_ref, normed_ref, qkv_ref, ctx_ref, w_held, wo_held, sems) = refs[:4], refs[4:]
    wait = start_weights(w_ref, w_held, sems, 0)
    last = pltpu.make_async_copy(wo_ref.at[0], wo_held, sems.at[3 * D // STEP])
    last.start()
    perm = perm_ref[...]
    for t in range(2):
        x = x_ref[:, 2 * k + t].reshape(GROUP, D)
        load_tokens(perm, x, xp_ref, normed_ref, t * GROUP)
    project(normed_ref, w_held, qkv_ref, wait)
    low, high = masks()
    for line in range(4):
        rows = slice(line * LINE, line * LINE + LINE)
        for p in range(PAIRS):
            at = p * 128
            q, k_, v = (qkv_ref[rows, part + at : part + at + 128] for part in (0, D, 2 * D))
            ctx_ref[rows, at : at + 128] = attend(q, k_, v, low, high, None)
    last.wait()
    for at in range(0, D, STEP):
        columns = slice(at, at + STEP)
        y = jnp.dot(ctx_ref[...], wo_held[:, columns], preferred_element_type=F32)
        y = (xp_ref[:, columns].astype(F32) + y).astype(BF)
        for r in range(4):
            for s in range(4):
                row = (r * 4 + s) * 32
                outs[s][r, :, columns] = y[row : row + 32]


def time_block(perm, lines, w_triple, w_out, k):
    tokens = 512
    return call(
        functools.partial(time_kernel, k=k),
        [perm, lines],
        [w_triple, w_out],
        [(4, 32, D)] * 4,
        [(tokens, D), (tokens, D), (tokens, 3 * D), (tokens, D), (D, 3 * D), (D, D)],
        cost(tokens, 4, tokens),
        f"time_block_{k}",
    )


def load_rows(pieces, xp_ref, normed_ref, start):
    frame = 4 * len(pieces)
    span = 8 * frame
    o = lax.broadcasted_iota(jnp.int32, (span, span), 0)
    i = lax.broadcasted_iota(jnp.int32, (span, span), 1)
    perm = ((o % frame) * 8 + o // frame == i).astype(F32).astype(BF)
    for n in range(4):
        x = [piece[r, n * 8 : n * 8 + 8, :] for piece in pieces for r in range(4)]
        load_tokens(perm, jnp.concatenate(x, axis=0), xp_ref, normed_ref, start + n * span)


EARLY = 768
LATE = 256


def early_kernel(*refs):
    pieces, w_ref, qkv_ref, xp_ref = refs[:6], refs[6], refs[7], refs[8]
    normed_ref, w_held, sems = refs[9:]
    wait = start_weights(w_ref, w_held, sems, 1)
    load_rows(pieces[:4], xp_ref, normed_ref, 0)
    load_rows(pieces[4:], xp_ref, normed_ref, 512)
    project(normed_ref, w_held, qkv_ref, wait)


def early(pieces, w_triple):
    return call(
        early_kernel,
        pieces,
        [w_triple],
        [(EARLY, 3 * D), (EARLY, D)],
        [(EARLY, D), (D, 3 * D)],
        cost(EARLY, 3, 0),
        "early",
        EARLY_LIMIT,
    )


def height_kernel(*refs):
    perm_ref, qkv_a, xp_a, pieces, w_ref, wo_ref, y_ref = *refs[:3], refs[3:5], *refs[5:8]
    xp_b, normed_ref, qkv_b, ctx_ref, w_held, wo_held, sems = refs[8:]
    wait = start_weights(w_ref, w_held, sems, 1)
    last = pltpu.make_async_copy(wo_ref.at[1], wo_held, sems.at[3 * D // STEP])
    last.start()
    load_rows(pieces, xp_b, normed_ref, 0)
    project(normed_ref, w_held, qkv_b, wait)

    def run(early, late, i, columns):
        at = lambda base, size: pl.ds(pl.multiple_of(base + i * size, size), size)
        parts = [early[at(0, 64), columns], early[at(512, 32), columns], late[at(0, 32), columns]]
        return jnp.concatenate(parts, axis=0)

    def frame(shape, axis):
        t = lax.broadcasted_iota(jnp.int32, shape, axis) % LINE
        return jnp.where(t < 64, t // 16, t % 32 // 8)

    low, high = masks()
    same = frame((2 * LINE, LINE), 0) == frame((2 * LINE, LINE), 1)

    @pl.loop(0, 8 // UNROLL)
    def _(n):
        for j in range(UNROLL):
            i = n * UNROLL + j
            rows = pl.ds(pl.multiple_of(i * LINE, LINE), LINE)
            for at in range(0, D, 128):
                q, k, v = (
                    run(qkv_a, qkv_b, i, slice(part + at, part + at + 128))
                    for part in (0, D, 2 * D)
                )
                ctx_ref[rows, at : at + 128] = attend(q, k, v, low, high, same)

    last.wait()
    for at in range(0, D, STEP):
        columns = slice(at, at + STEP)
        y = jnp.dot(ctx_ref[...], wo_held[:, columns], preferred_element_type=F32)
        for n in range(4):
            x = jnp.concatenate([run(xp_a, xp_b, i, columns) for i in (2 * n, 2 * n + 1)], axis=0)
            z = x.astype(F32) + y[n * GROUP : n * GROUP + GROUP]
            z = jnp.dot(perm_ref[...], z.astype(BF), preferred_element_type=F32).astype(BF)
            y_ref[n * 8 : n * 8 + 8, :, columns] = z.reshape(8, 32, STEP)


def height_block(perm, qkv_a, xp_a, pieces, w_triple, w_out):
    return call(
        height_kernel,
        [perm, qkv_a, xp_a, *pieces],
        [w_triple, w_out],
        [(32, 32, D)],
        [(LATE, D), (LATE, D), (LATE, 3 * D), (1024, D), (D, 3 * D), (D, D)],
        cost(1024, 3, 1024),
        "height_block",
        HEIGHT_LIMIT,
    )[0]


UNROLL = 8


def on_device(video, w_triple, w_out):
    g = lax.axis_index("grp")
    o = jnp.arange(GROUP)
    want = (o % 32) * 8 + (o // 128) * 4 + (((o // 32) % 4) ^ g)
    perm0 = permutation(want, o)
    m, s, chunk, r = o // 32, ((o // 8) % 4) ^ g, (o // 4) % 2, o % 4
    first = (m % 4) * 16 + s * 4 + r
    second = 64 + (s // 2) * 32 + (m % 4) * 8 + (s % 2) * 4 + r
    perm1 = permutation((m // 4) * LINE + jnp.where(chunk == 0, first, second), o)

    video, perm0, perm1 = lax.optimization_barrier((video, perm0, perm1))
    lines = lax.all_to_all(to_columns(video), "mem", split_axis=0, concat_axis=0, tiled=True)
    pieces = []
    for k in range(2):
        outs = time_block(perm0, lines, w_triple, w_out, k)
        pieces.append(
            [outs[0]]
            + [lax.ppermute(outs[s], "grp", [(i, i ^ s) for i in range(4)]) for s in range(1, 4)]
        )
        if k == 0:
            lines, pieces[0][0] = lax.optimization_barrier((lines, pieces[0][0]))
    qkv, xp = early(pieces[0] + pieces[1][:2], w_triple)
    done = height_block(perm1, qkv, xp, pieces[1][2:], w_triple, w_out)
    done = lax.all_to_all(
        done.reshape(128, 8, D), ("mem", "grp"), split_axis=0, concat_axis=0, tiled=True
    )
    return to_tokens(done.reshape(32, 4, 8, D))


def solution(mesh):
    return jax.shard_map(
        on_device,
        mesh=mesh,
        in_specs=(P("mem", "grp", None, None), P(), P()),
        out_specs=P("mem", "grp", None, None),
        check_vma=False,
    )
```
